32 devices in a mesh: vir: 8 (over z, y), occ: 4 (over x, core).
Axes of the slice: x: 2, y: 2, z: 4, core: 2. Of those that a mesh axis runs over, the one named last changes fastest.
Arguments:
- tiles: float32 [4096, 128, 128], P('vir'), may hold values from -0.02734375 to 0.02734375
- tile_slot: int32 [4096], P('vir'), may hold values from 0 to 2048, as said below
- amplitudes: float32 [262144, 1024], P('vir', 'occ'), may hold values from -6 to 6
- occ_energy: float32 [32], replicated, may hold values from -2 to -0.5
- vir_energy: float32 [32], replicated, may hold values from 0.5 to 3
Outputs:
- update: float32 [1024, 1024], P('vir', 'occ')
The draws below stay inside these ranges and needn't reach their ends.
Inputs may be any that keep to these rules, and one draw needn't show every extreme that they name: `tile_slot`: for each index v of vir, the slots v * 512 to v * 512 + 511 name distinct block positions below 2048, live slots first, then the empty value 8 * 256; each index has 128 or more live slots and some index has all 512 live.
All inputs are finite; a program needn't handle non-finite values.
Results may differ from the reference program's by a relative error of at most 0.0003.
Values sent between devices are 32-bit elements; how exact they have to be, the bound alone decides.
A program may use at most 320 MiB of HBM per device.

```python
import jax
import jax.numpy as jnp
from jax import lax

NV = 512
NO = 32
NW = 32
TILE = 128
NVP = 262144
NOP = 1024
ROW_BLOCKS = 8
COL_BLOCKS = 256
CAP = 512
N_VIR = 8


def draw_tile_slot(key, part):
    total_tiles = ROW_BLOCKS * COL_BLOCKS
    keys = jax.random.split(jax.random.fold_in(key, 11), N_VIR)

    def one_order(sub_key):
        return jax.random.permutation(sub_key, total_tiles)[:CAP]
    orders = jax.vmap(one_order)(keys)
    counts = jax.random.randint(jax.random.fold_in(key, 12), (N_VIR,), CAP // 4, CAP + 1)
    fullest = jax.random.randint(jax.random.fold_in(key, 13), (), 0, N_VIR)
    counts = jnp.where(jnp.arange(N_VIR) == fullest, CAP, counts)
    live = jnp.arange(CAP)[None, :] < counts[:, None]
    return jnp.where(live, orders, total_tiles).astype(jnp.int32).reshape(N_VIR * CAP)


def steps_of(own_key, extent, cuts, least, high):
    loudness = 1.0
    for position, parts in cuts:
        heights = jax.random.uniform(jax.random.fold_in(jax.random.fold_in(own_key, 6), position), (parts,), jnp.float32, least / len(cuts), high / len(cuts))
        loudness = loudness * jnp.repeat(jnp.exp(heights), extent[position] // parts).reshape((-1,) + (1,) * (len(extent) - 1 - position))
    return loudness


def noise(rng, dims, width, most, pieces=(), dtype=jnp.bfloat16):
    values = jax.random.normal(rng, dims, jnp.float32) * width
    if len(pieces) > 0:
        values = steps_of(rng, dims, pieces, -0.22, 0.18) * values
    return jnp.clip(values, min=-most, max=most).astype(dtype)


def setup_inputs(seed: int = 0) -> dict:
    streams_of = jax.random.split(jax.random.key(seed), 6)
    tiles = noise(streams_of[0], (N_VIR * CAP, TILE, TILE), (NV * NV // 5) ** -0.5, 0.02734375, ((0, 8),), jnp.float32)
    tile_slot = draw_tile_slot(jax.random.fold_in(streams_of[5], 71), 0)
    amplitudes = noise(streams_of[2], (NVP, NOP), 1.0, 6.0, ((0, 8), (1, 4)), jnp.float32)
    occ_energy = jnp.clip(jax.random.uniform(streams_of[3], (NO,), jnp.float32, -2.0, -0.5), -2.0, -0.5)
    vir_energy = jnp.clip(jax.random.uniform(streams_of[4], (NW,), jnp.float32, 0.5, 3.0), 0.5, 3.0)
    return dict(tiles=tiles, tile_slot=tile_slot, amplitudes=amplitudes, occ_energy=occ_energy, vir_energy=vir_energy)


def reference(tiles, tile_slot, amplitudes, occ_energy, vir_energy):
    row_blocks = NW * NW // TILE
    col_blocks = NV * NV // (N_VIR * TILE)
    pair_count = NO * NO
    tile_sets = tiles.reshape(N_VIR, CAP, TILE, TILE)
    slot_sets = tile_slot.reshape(N_VIR, CAP)
    amp_sets = amplitudes.reshape(N_VIR, col_blocks, TILE, pair_count)

    def add_device(running_sum, inputs):
        tile_set, slots, amp_block = inputs
        row_ids = (slots // col_blocks).astype(jnp.int32)
        col_ids = (slots % col_blocks).astype(jnp.int32)
        picked = amp_block[col_ids]
        products = jnp.einsum("kxy,kyn->kxn", tile_set, picked, precision=lax.Precision.HIGHEST)
        summed = jax.ops.segment_sum(products, row_ids, num_segments=row_blocks + 1)
        return running_sum + summed[:row_blocks], None

    start = jnp.zeros((row_blocks, TILE, pair_count), jnp.float32)
    ladder, unused = lax.scan(add_device, start, (tile_sets, slot_sets, amp_sets))
    pair_sums = ladder.reshape(NW, NW, NO, NO)
    mirror = pair_sums.transpose(1, 0, 3, 2)
    denominator = (occ_energy[None, None, :, None] + occ_energy[None, None, None, :]
                   - vir_energy[:, None, None, None] - vir_energy[None, :, None, None])
    return ((pair_sums + mirror) / denominator).reshape(NW * NW, NO * NO)
```

```python
import functools

import jax
import jax.numpy as jnp
from jax import lax
from jax.experimental import pallas as pl
from jax.experimental.pallas import tpu as pltpu
from jax.sharding import PartitionSpec as P

NO = 32
NW = 32
GROUP = 4
UNROLL = 4
TILE_DEPTH = 4
AMP_DEPTH = 6
MIB = 1024 * 1024


def split_two(x):
    high = x.astype(jnp.bfloat16)
    low = (x - high.astype(jnp.float32)).astype(jnp.bfloat16)
    return high, low


def ladder_kernel(
    row_blocks, slots_ref, slot_vec_ref, tiles_hbm, amp_hbm, out_ref,
    amp_high, amp_low, stage, ring, place_slot, place_col, group_row, cursor,
    amp_sem, ring_sem,
):
    slot_count, tile, _ = tiles_hbm.shape
    cd, width = amp_hbm.shape
    col_blocks = cd // tile
    chunk = stage.shape[1]
    chunks = cd // chunk
    per_chunk = slot_count // chunks
    batch = GROUP * UNROLL

    def amp_copy(i):
        slot = lax.rem(i, AMP_DEPTH)
        return pltpu.make_async_copy(
            amp_hbm.at[pl.ds(pl.multiple_of(i * chunk, chunk), chunk)],
            stage.at[slot], amp_sem.at[slot],
        )

    for i in range(min(AMP_DEPTH - 1, chunks)):
        amp_copy(i).start()

    slot_vec = slot_vec_ref[...]
    start = jnp.int32(0)
    for r in range(row_blocks):
        inside = (slot_vec >= r * col_blocks) & (slot_vec < (r + 1) * col_blocks)
        count = jnp.sum(jnp.where(inside, 1.0, 0.0)).astype(jnp.int32)
        cursor[r] = start
        start = start + ((count + GROUP - 1) // GROUP) * GROUP
        for t in range(1, GROUP):
            at = jnp.maximum(start - t, 0)
            place_slot[at] = 0
            place_col[at] = col_blocks
    total = start
    for t in range(batch):
        place_slot[total + t] = 0
        place_col[total + t] = col_blocks
    for t in range(UNROLL):
        group_row[total // GROUP + t] = 0
    cursor[row_blocks] = total + batch
    steps = (total + batch - 1) // batch

    out_ref[...] = jnp.zeros_like(out_ref)
    amp_high[pl.ds(cd, tile), :] = jnp.zeros((tile, width), jnp.bfloat16)
    amp_low[pl.ds(cd, tile), :] = jnp.zeros((tile, width), jnp.bfloat16)

    def load_chunk(i, carry):
        amp_copy(i).wait()

        @pl.when(i + AMP_DEPTH - 1 < chunks)
        def _():
            amp_copy(i + AMP_DEPTH - 1).start()

        high, low = split_two(stage[lax.rem(i, AMP_DEPTH)])
        rows = pl.ds(pl.multiple_of(i * chunk, chunk), chunk)
        amp_high[rows, :] = high
        amp_low[rows, :] = low
        for q in range(per_chunk):
            k = i * per_chunk + q
            s = slots_ref[k]
            r = lax.div(s, jnp.int32(col_blocks))
            at = cursor[r]
            place_slot[at] = k
            place_col[at] = s - r * col_blocks
            group_row[at // GROUP] = r
            cursor[r] = at + 1
        return carry

    lax.fori_loop(0, chunks, load_chunk, 0)

    def start_tiles(i):
        slot = lax.rem(i, TILE_DEPTH)
        for t in range(batch):
            pltpu.make_async_copy(
                tiles_hbm.at[place_slot[i * batch + t]],
                ring.at[slot, t], ring_sem.at[slot],
            ).start()

    def wait_tiles(i):
        slot = lax.rem(i, TILE_DEPTH)
        pltpu.make_async_copy(
            tiles_hbm.at[pl.ds(0, batch)], ring.at[slot], ring_sem.at[slot]
        ).wait()

    for i in range(TILE_DEPTH - 1):
        @pl.when(i < steps)
        def _(i=i):
            start_tiles(jnp.int32(i))

    def multiply(i, carry):
        wait_tiles(i)

        @pl.when(i + TILE_DEPTH - 1 < steps)
        def _():
            start_tiles(i + TILE_DEPTH - 1)

        slot = lax.rem(i, TILE_DEPTH)
        products = []
        for u in range(UNROLL):
            highs, lows, amp_highs, amp_lows = [], [], [], []
            for t in range(GROUP):
                at = u * GROUP + t
                high, low = split_two(ring[slot, at])
                first = pl.multiple_of(place_col[i * batch + at] * tile, tile)
                highs.append(high)
                lows.append(low)
                amp_highs.append(amp_high[pl.ds(first, tile), :])
                amp_lows.append(amp_low[pl.ds(first, tile), :])
            left = jnp.concatenate(highs + lows + highs, axis=1)
            right = jnp.concatenate(amp_highs + amp_highs + amp_lows, axis=0)
            products.append(jnp.dot(left, right, preferred_element_type=jnp.float32))
        for u in range(UNROLL):
            first = pl.multiple_of(group_row[i * UNROLL + u] * tile, tile)
            out_ref[pl.ds(first, tile), :] += products[u]
        return carry

    lax.fori_loop(0, steps, multiply, 0)


def ladder_partial(tiles, tile_slot, amplitudes, row_blocks):
    slot_count, tile, _ = tiles.shape
    cd, width = amplitudes.shape
    chunk = min(512, cd)
    batch = GROUP * UNROLL
    lanes = min(128, slot_count)
    places = 2 * slot_count + row_blocks * GROUP + 2 * batch
    flops = 6 * slot_count * tile * tile * width
    return pl.pallas_call(
        functools.partial(ladder_kernel, row_blocks),
        out_shape=jax.ShapeDtypeStruct((row_blocks * tile, width), jnp.float32),
        in_specs=[
            pl.BlockSpec(memory_space=pltpu.SMEM),
            pl.BlockSpec(memory_space=pltpu.VMEM),
            pl.BlockSpec(memory_space=pl.ANY),
            pl.BlockSpec(memory_space=pl.ANY),
        ],
        out_specs=pl.BlockSpec(memory_space=pltpu.VMEM),
        scratch_shapes=[
            pltpu.VMEM((cd + tile, width), jnp.bfloat16),
            pltpu.VMEM((cd + tile, width), jnp.bfloat16),
            pltpu.VMEM((AMP_DEPTH, chunk, width), jnp.float32),
            pltpu.VMEM((TILE_DEPTH, batch, tile, tile), jnp.float32),
            pltpu.SMEM((places,), jnp.int32),
            pltpu.SMEM((places,), jnp.int32),
            pltpu.SMEM((places,), jnp.int32),
            pltpu.SMEM((row_blocks + 1,), jnp.int32),
            pltpu.SemaphoreType.DMA((AMP_DEPTH,)),
            pltpu.SemaphoreType.DMA((TILE_DEPTH,)),
        ],
        compiler_params=pltpu.CompilerParams(vmem_limit_bytes=56 * MIB),
        cost_estimate=pl.CostEstimate(
            flops=flops,
            bytes_accessed=4 * (tiles.size + amplitudes.size),
            transcendentals=0,
        ),
    )(tile_slot, tile_slot.reshape(slot_count // lanes, lanes), tiles, amplitudes)


def per_device(tiles, tile_slot, amplitudes, occ_energy, vir_energy):
    ij_dev = amplitudes.shape[1]
    pair_rows = NW * NW
    row_blocks = pair_rows // tiles.shape[1]
    occ_local = ij_dev // NO
    own_rows = pair_rows // lax.axis_size("vir")
    partial_sum = ladder_partial(tiles, tile_slot, amplitudes, row_blocks)
    swapped = partial_sum.reshape(NW, NW, ij_dev).transpose(1, 0, 2).reshape(pair_rows, ij_dev)
    moved = lax.all_to_all(
        swapped.reshape(pair_rows, occ_local, NO), "occ", split_axis=2, concat_axis=1, tiled=True
    )
    numerator = partial_sum + moved.transpose(0, 2, 1).reshape(pair_rows, ij_dev)
    total = lax.psum_scatter(numerator, "vir", scatter_dimension=0, tiled=True)
    row_ids = lax.axis_index("vir") * own_rows + lax.broadcasted_iota(jnp.int32, (own_rows,), 0)
    first_orb = row_ids // NW
    second_orb = row_ids % NW
    orbital = lax.broadcasted_iota(jnp.int32, (NW,), 0)
    energy_first = jnp.sum(
        jnp.where(first_orb[:, None] == orbital[None, :], vir_energy[None, :], 0.0), axis=1
    )
    energy_second = jnp.sum(
        jnp.where(second_orb[:, None] == orbital[None, :], vir_energy[None, :], 0.0), axis=1
    )
    own_occ = lax.dynamic_slice_in_dim(occ_energy, lax.axis_index("occ") * occ_local, occ_local)
    denominator = (
        own_occ[None, :, None]
        + occ_energy[None, None, :]
        - energy_first[:, None, None]
        - energy_second[:, None, None]
    )
    return (total.reshape(own_rows, occ_local, NO) / denominator).reshape(own_rows, ij_dev)


def solution(mesh):
    in_specs = (P("vir", None, None), P("vir"), P("vir", "occ"), P(), P())
    out_specs = P("vir", "occ")
    return jax.shard_map(
        per_device, mesh=mesh, in_specs=in_specs, out_specs=out_specs, check_vma=False
    )
```

```python
import functools

import jax
import jax.numpy as jnp
from jax import lax
from jax.experimental import pallas as pl
from jax.experimental.pallas import tpu as pltpu
from jax.sharding import PartitionSpec as P

NO = 32
NW = 32
GROUP = 4
UNROLL = 4
TILE_DEPTH = 5
AMP_PARTS = 8
MIB = 1024 * 1024


def split_two(x):
    high = x.astype(jnp.bfloat16)
    low = (x - high.astype(jnp.float32)).astype(jnp.bfloat16)
    return high, low


def ladder_kernel(
    row_blocks, slots_ref, slot_vec_ref, tiles_hbm, amp_hbm, out_ref,
    amp, ring, place_slot, place_col, group_row, cursor, amp_sem, ring_sem,
):
    slot_count, tile, _ = tiles_hbm.shape
    cd, width = amp_hbm.shape
    col_blocks = cd // tile
    batch = GROUP * UNROLL
    part = cd // AMP_PARTS

    def amp_copy(i):
        rows = pl.ds(i * part, part)
        return pltpu.make_async_copy(amp_hbm.at[rows], amp.at[rows], amp_sem.at[i])

    for i in range(AMP_PARTS):
        amp_copy(i).start()

    slot_vec = slot_vec_ref[...]
    start = jnp.int32(0)
    for r in range(row_blocks):
        inside = (slot_vec >= r * col_blocks) & (slot_vec < (r + 1) * col_blocks)
        count = jnp.sum(jnp.where(inside, 1.0, 0.0)).astype(jnp.int32)
        cursor[r] = start
        start = start + ((count + GROUP - 1) // GROUP) * GROUP
        for t in range(1, GROUP):
            at = jnp.maximum(start - t, 0)
            place_slot[at] = 0
            place_col[at] = col_blocks
    total = start
    for t in range(batch):
        place_slot[total + t] = 0
        place_col[total + t] = col_blocks
    for t in range(UNROLL):
        group_row[total // GROUP + t] = 0
    cursor[row_blocks] = total + batch
    steps = (total + batch - 1) // batch

    out_ref[...] = jnp.zeros_like(out_ref)
    amp[pl.ds(cd, tile), :] = jnp.zeros((tile, width), jnp.float32)

    def place(i, carry):
        for q in range(8):
            k = i * 8 + q
            s = slots_ref[k]
            r = lax.div(s, jnp.int32(col_blocks))
            at = cursor[r]
            place_slot[at] = k
            place_col[at] = s - r * col_blocks
            group_row[at // GROUP] = r
            cursor[r] = at + 1
        return carry

    lax.fori_loop(0, slot_count // 8, place, 0)

    def start_tiles(i):
        slot = lax.rem(i, TILE_DEPTH)
        for t in range(batch):
            pltpu.make_async_copy(
                tiles_hbm.at[place_slot[i * batch + t]],
                ring.at[slot, t], ring_sem.at[slot],
            ).start()

    def wait_tiles(i):
        slot = lax.rem(i, TILE_DEPTH)
        pltpu.make_async_copy(
            tiles_hbm.at[pl.ds(0, batch)], ring.at[slot], ring_sem.at[slot]
        ).wait()

    for i in range(TILE_DEPTH - 1):
        @pl.when(i < steps)
        def _(i=i):
            start_tiles(jnp.int32(i))
    for i in range(AMP_PARTS):
        amp_copy(i).wait()

    def multiply(i, carry):
        wait_tiles(i)

        @pl.when(i + TILE_DEPTH - 1 < steps)
        def _():
            start_tiles(i + TILE_DEPTH - 1)

        slot = lax.rem(i, TILE_DEPTH)
        products = []
        for u in range(UNROLL):
            highs, lows, amp_highs, amp_lows = [], [], [], []
            for t in range(GROUP):
                at = u * GROUP + t
                high, low = split_two(ring[slot, at])
                first = pl.multiple_of(place_col[i * batch + at] * tile, tile)
                amp_high, amp_low = split_two(amp[pl.ds(first, tile), :])
                highs.append(high)
                lows.append(low)
                amp_highs.append(amp_high)
                amp_lows.append(amp_low)
            left = jnp.concatenate(highs + lows + highs, axis=1)
            right = jnp.concatenate(amp_highs + amp_highs + amp_lows, axis=0)
            products.append(jnp.dot(left, right, preferred_element_type=jnp.float32))
        for u in range(UNROLL):
            first = pl.multiple_of(group_row[i * UNROLL + u] * tile, tile)
            out_ref[pl.ds(first, tile), :] += products[u]
        return carry

    lax.fori_loop(0, steps, multiply, 0)


def ladder_partial(tiles, tile_slot, amplitudes, row_blocks):
    slot_count, tile, _ = tiles.shape
    cd, width = amplitudes.shape
    batch = GROUP * UNROLL
    lanes = min(128, slot_count)
    places = 2 * slot_count + row_blocks * GROUP + 2 * batch
    flops = 6 * slot_count * tile * tile * width
    return pl.pallas_call(
        functools.partial(ladder_kernel, row_blocks),
        out_shape=jax.ShapeDtypeStruct((row_blocks * tile, width), jnp.float32),
        in_specs=[
            pl.BlockSpec(memory_space=pltpu.SMEM),
            pl.BlockSpec(memory_space=pltpu.VMEM),
            pl.BlockSpec(memory_space=pl.ANY),
            pl.BlockSpec(memory_space=pl.ANY),
        ],
        out_specs=pl.BlockSpec(memory_space=pltpu.VMEM),
        scratch_shapes=[
            pltpu.VMEM((cd + tile, width), jnp.float32),
            pltpu.VMEM((TILE_DEPTH, batch, tile, tile), jnp.float32),
            pltpu.SMEM((places,), jnp.int32),
            pltpu.SMEM((places,), jnp.int32),
            pltpu.SMEM((places,), jnp.int32),
            pltpu.SMEM((row_blocks + 1,), jnp.int32),
            pltpu.SemaphoreType.DMA((AMP_PARTS,)),
            pltpu.SemaphoreType.DMA((TILE_DEPTH,)),
        ],
        compiler_params=pltpu.CompilerParams(vmem_limit_bytes=56 * MIB),
        cost_estimate=pl.CostEstimate(
            flops=flops,
            bytes_accessed=4 * (tiles.size + amplitudes.size),
            transcendentals=0,
        ),
    )(tile_slot, tile_slot.reshape(slot_count // lanes, lanes), tiles, amplitudes)


def one_hot(shape, want):
    row = lax.broadcasted_iota(jnp.int32, shape, 0)
    col = lax.broadcasted_iota(jnp.int32, shape, 1)
    return jnp.where(want(row, col), 1.0, 0.0)


def mirror_fits(vir_size, occ_size):
    if vir_size % 2 or NW % vir_size or NO % occ_size:
        return False
    a_own, i_own = NW // vir_size, NO // occ_size
    if 128 % (i_own * i_own) or a_own * a_own * i_own * i_own != 1024:
        return False
    return a_own % (128 // (i_own * i_own)) == 0


def exchange_kernel(
    vir_size, occ_size, partial_ref, out_ref,
    pair_in, line_out, line_in, outgoing, incoming,
    rows_out, cols_out, rows_in, cols_in,
    pair_send, pair_recv, line_send, line_recv, mirror_send, mirror_recv,
):
    exact = lax.Precision.HIGHEST
    own_rows, width = out_ref.shape
    a_own, i_own = NW // vir_size, NO // occ_size
    folds = 128 // (i_own * i_own)
    a_fold = a_own // folds
    devices = vir_size * occ_size
    line = vir_size // 2
    vir = lax.axis_index("vir")
    occ = lax.axis_index("occ")
    me = vir * occ_size + occ
    z, y = vir // 2, vir % 2

    barrier = pltpu.get_barrier_semaphore()

    def greet(k, carry):
        other = (me + k) % devices
        pl.semaphore_signal(
            barrier, inc=1,
            device_id={"vir": other // occ_size, "occ": other % occ_size},
            device_id_type=pl.DeviceIdType.MESH,
        )
        return carry

    lax.fori_loop(1, devices, greet, 0)
    pl.semaphore_wait(barrier, devices - 1)

    def block(z_to, y_to):
        first = (z_to * 2 + y_to) * own_rows
        return pl.ds(pl.multiple_of(first, own_rows), own_rows)

    middle = line // 2
    order = sorted(range(1, line), key=lambda s: abs(s - middle)) + [0]
    pair_copies = {}
    for s in order:
        pair_copies[s] = pltpu.make_async_remote_copy(
            src_ref=partial_ref.at[block((z + s) % line, 1 - y)],
            dst_ref=pair_in.at[s],
            send_sem=pair_send.at[s], recv_sem=pair_recv.at[s],
            device_id={"vir": z * 2 + 1 - y, "occ": occ},
            device_id_type=pl.DeviceIdType.MESH,
        )
        pair_copies[s].start()

    half = vir_size * a_fold * a_own
    lanes = occ_size * 128
    square = i_own * i_own

    def place_rows(at, r):
        fold, rest = at // half, at % half
        v, p, b = rest // (a_fold * a_own), (rest // a_own) % a_fold, rest % a_own
        return r == (fold * a_fold + p) * NW + v * a_own + b

    def return_rows(r, at):
        fold, rest = at // half, at % half
        v, p, b = rest // (a_fold * a_own), (rest // a_own) % a_fold, rest % a_own
        return r == b * NW + v * a_own + fold * a_fold + p

    rows_out[...] = one_hot((own_rows, own_rows), place_rows)
    rows_in[...] = one_hot((own_rows, own_rows), return_rows)
    for fold in range(folds):
        def place_cols(c, at):
            o, rest = at // 128, at % 128
            j, i = (rest % square) // i_own, rest % i_own
            return (rest // square == fold) & (c == i * NO + o * i_own + j)

        def return_cols(at, c):
            o, rest = at // 128, at % 128
            j, i = (rest % square) // i_own, rest % i_own
            return (rest // square == fold) & (c == j * NO + o * i_own + i)

        cols_out[fold] = one_hot((width, lanes), place_cols)
        cols_in[fold] = one_hot((lanes, width), return_cols)

    line_copies = {}
    for s in order:
        pair_copies[s].wait_recv()
        if s == 0:
            continue
        line_out[s] = partial_ref[block((z + s) % line, y), :] + pair_in[s]
        line_copies[s] = pltpu.make_async_remote_copy(
            src_ref=line_out.at[s], dst_ref=line_in.at[s],
            send_sem=line_send.at[s], recv_sem=line_recv.at[s],
            device_id={"vir": ((z + s) % line) * 2 + y, "occ": occ},
            device_id_type=pl.DeviceIdType.MESH,
        )
        line_copies[s].start()
    total = partial_ref[block(z, y), :] + pair_in[0]
    for s in order[:-1]:
        line_copies[s].wait_recv()
        total = total + line_in[s]

    moved = jnp.dot(rows_out[...], total, precision=exact, preferred_element_type=jnp.float32)
    folded = jnp.zeros((half, lanes), jnp.float32)
    for fold in range(folds):
        folded = folded + jnp.dot(
            moved[fold * half:(fold + 1) * half], cols_out[fold],
            precision=exact, preferred_element_type=jnp.float32,
        )
    outgoing[...] = folded

    def cell(ref, v, o):
        return ref.at[
            pl.ds(pl.multiple_of(v * 8, 8), 8), pl.ds(pl.multiple_of(o * 128, 128), 128)
        ]

    def mirror_copy(k):
        other = (me + k) % devices
        v, o = other // occ_size, other % occ_size
        return pltpu.make_async_remote_copy(
            src_ref=cell(outgoing, v, o), dst_ref=cell(incoming, vir, occ),
            send_sem=mirror_send.at[k], recv_sem=mirror_recv.at[k],
            device_id={"vir": v, "occ": o},
            device_id_type=pl.DeviceIdType.MESH,
        )

    def send(k, carry):
        mirror_copy(k).start()
        return carry

    lax.fori_loop(1, devices, send, 0)
    cell(incoming, vir, occ)[...] = cell(outgoing, vir, occ)[...]

    def receive(k, carry):
        other = (me + devices - k) % devices
        v, o = other // occ_size, other % occ_size
        pltpu.make_async_remote_copy(
            src_ref=cell(outgoing, v, o), dst_ref=cell(incoming, v, o),
            send_sem=mirror_send.at[k], recv_sem=mirror_recv.at[k],
            device_id={"vir": v, "occ": o},
            device_id_type=pl.DeviceIdType.MESH,
        ).wait_recv()
        return carry

    lax.fori_loop(1, devices, receive, 0)
    unfolded = [
        jnp.dot(incoming[...], cols_in[fold], precision=exact, preferred_element_type=jnp.float32)
        for fold in range(folds)
    ]
    back = jnp.dot(
        rows_in[...], jnp.concatenate(unfolded, axis=0),
        precision=exact, preferred_element_type=jnp.float32,
    )
    out_ref[...] = total + back

    for s in order:
        pair_copies[s].wait_send()
        if s:
            line_copies[s].wait_send()

    def sent(k, carry):
        mirror_copy(k).wait_send()
        return carry

    lax.fori_loop(1, devices, sent, 0)


def exchange(partial_sum):
    vir_size, occ_size = lax.axis_size("vir"), lax.axis_size("occ")
    pair_rows, width = partial_sum.shape
    own_rows = pair_rows // vir_size
    line = vir_size // 2
    folds = 128 // (NO // occ_size) ** 2
    lanes = occ_size * 128
    block = (line, own_rows, width)
    devices = vir_size * occ_size
    return pl.pallas_call(
        functools.partial(exchange_kernel, vir_size, occ_size),
        out_shape=jax.ShapeDtypeStruct((own_rows, width), jnp.float32),
        in_specs=[pl.BlockSpec(memory_space=pltpu.VMEM)],
        out_specs=pl.BlockSpec(memory_space=pltpu.VMEM),
        scratch_shapes=[
            pltpu.VMEM(block, jnp.float32),
            pltpu.VMEM(block, jnp.float32),
            pltpu.VMEM(block, jnp.float32),
            pltpu.VMEM((vir_size * 8, lanes), jnp.float32),
            pltpu.VMEM((vir_size * 8, lanes), jnp.float32),
            pltpu.VMEM((own_rows, own_rows), jnp.float32),
            pltpu.VMEM((folds, width, lanes), jnp.float32),
            pltpu.VMEM((own_rows, own_rows), jnp.float32),
            pltpu.VMEM((folds, lanes, width), jnp.float32),
            pltpu.SemaphoreType.DMA((line,)),
            pltpu.SemaphoreType.DMA((line,)),
            pltpu.SemaphoreType.DMA((line,)),
            pltpu.SemaphoreType.DMA((line,)),
            pltpu.SemaphoreType.DMA((devices,)),
            pltpu.SemaphoreType.DMA((devices,)),
        ],
        compiler_params=pltpu.CompilerParams(
            collective_id=0, has_side_effects=True, vmem_limit_bytes=24 * MIB
        ),
    )(partial_sum)


def exchange_by_collectives(partial_sum):
    pair_rows, ij_dev = partial_sum.shape
    occ_local = ij_dev // NO
    swapped = partial_sum.reshape(NW, NW, ij_dev).transpose(1, 0, 2).reshape(pair_rows, ij_dev)
    moved = lax.all_to_all(
        swapped.reshape(pair_rows, occ_local, NO), "occ", split_axis=2, concat_axis=1, tiled=True
    )
    numerator = partial_sum + moved.transpose(0, 2, 1).reshape(pair_rows, ij_dev)
    return lax.psum_scatter(numerator, "vir", scatter_dimension=0, tiled=True)


def per_device(tiles, tile_slot, amplitudes, occ_energy, vir_energy):
    ij_dev = amplitudes.shape[1]
    pair_rows = NW * NW
    row_blocks = pair_rows // tiles.shape[1]
    own_rows = pair_rows // lax.axis_size("vir")
    row_ids = lax.axis_index("vir") * own_rows + jnp.arange(own_rows)
    orbital = jnp.arange(NW)
    picks = (row_ids[:, None] // NW == orbital[None, :], row_ids[:, None] % NW == orbital[None, :])
    vir_pair = sum(jnp.sum(jnp.where(p, vir_energy[None, :], 0.0), axis=1) for p in picks)
    col_ids = lax.axis_index("occ") * ij_dev + jnp.arange(ij_dev)
    occupied = jnp.arange(NO)
    picks = (col_ids[None, :] // NO == occupied[:, None], col_ids[None, :] % NO == occupied[:, None])
    occ_pair = sum(jnp.sum(jnp.where(p, occ_energy[:, None], 0.0), axis=0) for p in picks)
    partial_sum = ladder_partial(tiles, tile_slot, amplitudes, row_blocks)
    if mirror_fits(lax.axis_size("vir"), lax.axis_size("occ")):
        numerator = exchange(partial_sum)
    else:
        numerator = exchange_by_collectives(partial_sum)
    return numerator / (occ_pair[None, :] - vir_pair[:, None])


def solution(mesh):
    in_specs = (P("vir", None, None), P("vir"), P("vir", "occ"), P(), P())
    out_specs = P("vir", "occ")
    return jax.shard_map(
        per_device, mesh=mesh, in_specs=in_specs, out_specs=out_specs, check_vma=False
    )
```

```python
import functools

import jax
import jax.numpy as jnp
from jax import lax
from jax.experimental import pallas as pl
from jax.experimental.pallas import tpu as pltpu
from jax.sharding import PartitionSpec as P

NO = 32
NW = 32
GROUP = 4
UNROLL = 4
TILE_DEPTH = 4
AMP_DEPTH = 5
MIB = 1024 * 1024


def split_two(x):
    high = x.astype(jnp.bfloat16)
    low = (x - high.astype(jnp.float32)).astype(jnp.bfloat16)
    return high, low


def quotient(x, n):
    if n & (n - 1) == 0:
        return x >> (n.bit_length() - 1)
    return x // n


def remainder(x, n):
    if n & (n - 1) == 0:
        return x & (n - 1)
    return x % n


def ladder_kernel(
    row_blocks, slots_ref, slot_vec_ref, tiles_hbm, amp_hbm, out_ref,
    amp_high, amp_low, stage, ring, places, cursor,
    amp_sem, ring_sem,
):
    slot_count, tile, _ = tiles_hbm.shape
    cd, width = amp_hbm.shape
    col_blocks = cd // tile
    chunk = stage.shape[1]
    chunks = cd // chunk
    per_chunk = slot_count // chunks
    batch = GROUP * UNROLL
    row_bits, col_bits = row_blocks.bit_length(), col_blocks.bit_length()

    def amp_copy(i):
        slot = lax.rem(i, AMP_DEPTH)
        return pltpu.make_async_copy(
            amp_hbm.at[pl.ds(pl.multiple_of(i * chunk, chunk), chunk)],
            stage.at[slot], amp_sem.at[slot],
        )

    for i in range(min(AMP_DEPTH - 1, chunks)):
        amp_copy(i).start()

    slot_vec = slot_vec_ref[...]
    start = jnp.int32(0)
    for r in range(row_blocks):
        inside = (slot_vec >= r * col_blocks) & (slot_vec < (r + 1) * col_blocks)
        count = jnp.sum(jnp.where(inside, 1.0, 0.0)).astype(jnp.int32)
        cursor[r] = start
        start = start + ((count + GROUP - 1) // GROUP) * GROUP
        for t in range(1, GROUP):
            at = jnp.maximum(start - t, 0)
            places[at] = col_blocks
    total = start
    for t in range(batch):
        places[total + t] = col_blocks
    cursor[row_blocks] = total + batch
    steps = (total + batch - 1) // batch

    out_ref[...] = jnp.zeros_like(out_ref)
    amp_high[pl.ds(cd, tile), :] = jnp.zeros((tile, width), jnp.bfloat16)
    amp_low[pl.ds(cd, tile), :] = jnp.zeros((tile, width), jnp.bfloat16)

    def load_chunk(i, carry):
        amp_copy(i).wait()

        @pl.when(i + AMP_DEPTH - 1 < chunks)
        def _():
            amp_copy(i + AMP_DEPTH - 1).start()

        high, low = split_two(stage[lax.rem(i, AMP_DEPTH)])
        rows = pl.ds(pl.multiple_of(i * chunk, chunk), chunk)
        amp_high[rows, :] = high
        amp_low[rows, :] = low
        for q in range(per_chunk):
            k = i * per_chunk + q
            s = slots_ref[k]
            r = quotient(s, col_blocks)
            at = cursor[r]
            places[at] = (((k << row_bits) + r) << col_bits) + (s - r * col_blocks)
            cursor[r] = at + 1
        return carry

    lax.fori_loop(0, chunks, load_chunk, 0)

    def start_tiles(i):
        slot = lax.rem(i, TILE_DEPTH)
        for t in range(batch):
            pltpu.make_async_copy(
                tiles_hbm.at[places[i * batch + t] >> (row_bits + col_bits)],
                ring.at[slot, t], ring_sem.at[slot],
            ).start()

    def wait_tiles(i):
        slot = lax.rem(i, TILE_DEPTH)
        pltpu.make_async_copy(
            tiles_hbm.at[pl.ds(0, batch)], ring.at[slot], ring_sem.at[slot]
        ).wait()

    for i in range(TILE_DEPTH - 1):
        @pl.when(i < steps)
        def _(i=i):
            start_tiles(jnp.int32(i))

    def multiply(i, carry):
        wait_tiles(i)

        @pl.when(i + TILE_DEPTH - 1 < steps)
        def _():
            start_tiles(i + TILE_DEPTH - 1)

        slot = lax.rem(i, TILE_DEPTH)
        products = []
        for u in range(UNROLL):
            highs, lows, amp_highs, amp_lows = [], [], [], []
            for t in range(GROUP):
                at = u * GROUP + t
                high, low = split_two(ring[slot, at])
                col = places[i * batch + at] & ((1 << col_bits) - 1)
                first = pl.multiple_of(col * tile, tile)
                highs.append(high)
                lows.append(low)
                amp_highs.append(amp_high[pl.ds(first, tile), :])
                amp_lows.append(amp_low[pl.ds(first, tile), :])
            left = jnp.concatenate(highs + lows + highs, axis=1)
            right = jnp.concatenate(amp_highs + amp_highs + amp_lows, axis=0)
            products.append(jnp.dot(left, right, preferred_element_type=jnp.float32))
        for u in range(UNROLL):
            row = (places[i * batch + u * GROUP] >> col_bits) & ((1 << row_bits) - 1)
            first = pl.multiple_of(row * tile, tile)
            out_ref[pl.ds(first, tile), :] += products[u]
        return carry

    lax.fori_loop(0, steps, multiply, 0)


def ladder_partial(tiles, tile_slot, amplitudes, row_blocks):
    slot_count, tile, _ = tiles.shape
    cd, width = amplitudes.shape
    chunk = min(1024, cd)
    batch = GROUP * UNROLL
    lanes = min(128, slot_count)
    places = 2 * slot_count + row_blocks * GROUP + 2 * batch
    flops = 6 * slot_count * tile * tile * width
    return pl.pallas_call(
        functools.partial(ladder_kernel, row_blocks),
        out_shape=jax.ShapeDtypeStruct((row_blocks * tile, width), jnp.float32),
        in_specs=[
            pl.BlockSpec(memory_space=pltpu.SMEM),
            pl.BlockSpec(memory_space=pltpu.VMEM),
            pl.BlockSpec(memory_space=pl.ANY),
            pl.BlockSpec(memory_space=pl.ANY),
        ],
        out_specs=pl.BlockSpec(memory_space=pltpu.VMEM),
        scratch_shapes=[
            pltpu.VMEM((cd + tile, width), jnp.bfloat16),
            pltpu.VMEM((cd + tile, width), jnp.bfloat16),
            pltpu.VMEM((AMP_DEPTH, chunk, width), jnp.float32),
            pltpu.VMEM((TILE_DEPTH, batch, tile, tile), jnp.float32),
            pltpu.SMEM((places,), jnp.int32),
            pltpu.SMEM((row_blocks + 1,), jnp.int32),
            pltpu.SemaphoreType.DMA((AMP_DEPTH,)),
            pltpu.SemaphoreType.DMA((TILE_DEPTH,)),
        ],
        compiler_params=pltpu.CompilerParams(vmem_limit_bytes=56 * MIB),
        cost_estimate=pl.CostEstimate(
            flops=flops,
            bytes_accessed=4 * (tiles.size + amplitudes.size),
            transcendentals=0,
        ),
    )(tile_slot, tile_slot.reshape(slot_count // lanes, lanes), tiles, amplitudes)


def one_hot(shape, want):
    row = lax.broadcasted_iota(jnp.int32, shape, 0)
    col = lax.broadcasted_iota(jnp.int32, shape, 1)
    return jnp.where(want(row, col), 1.0, 0.0).astype(jnp.bfloat16)


def three_terms(x):
    first = x.astype(jnp.bfloat16)
    rest = x - first.astype(jnp.float32)
    second = rest.astype(jnp.bfloat16)
    third = (rest - second.astype(jnp.float32)).astype(jnp.bfloat16)
    return [first, second, third]


def permute_rows(rows, x):
    width = x.shape[1]
    wide = jnp.dot(
        rows, jnp.concatenate(three_terms(x), axis=1), preferred_element_type=jnp.float32
    )
    return wide[:, :width] + wide[:, width:2 * width] + wide[:, 2 * width:]


def permute_cols(x, cols):
    depth = x.shape[0]
    tall = jnp.dot(
        jnp.concatenate(three_terms(x), axis=0), cols, preferred_element_type=jnp.float32
    )
    return tall[:depth] + tall[depth:2 * depth] + tall[2 * depth:]


def mirror_fits(vir_size, occ_size):
    if vir_size % 2 or NW % vir_size or NO % occ_size:
        return False
    a_own, i_own = NW // vir_size, NO // occ_size
    if 128 % (i_own * i_own) or a_own * a_own * i_own * i_own != 1024:
        return False
    return a_own % (128 // (i_own * i_own)) == 0


def exchange_kernel(
    vir_size, occ_size, partial_ref, out_ref,
    own, pair_in, line_out, line_in, outgoing, incoming,
    rows_out, cols_out, rows_in, cols_in,
    own_sem, pair_send, pair_recv, line_send, line_recv, mirror_send, mirror_recv,
):
    own_rows, width = out_ref.shape
    a_own, i_own = NW // vir_size, NO // occ_size
    folds = 128 // (i_own * i_own)
    a_fold = a_own // folds
    devices = vir_size * occ_size
    line = vir_size // 2
    vir = lax.axis_index("vir")
    occ = lax.axis_index("occ")
    z, y = vir // 2, vir % 2
    vir_to = [lax.rem(vir + k, vir_size) for k in range(vir_size)]
    vir_from = [lax.rem(vir + vir_size - k, vir_size) for k in range(vir_size)]
    occ_to = [lax.rem(occ + k, occ_size) for k in range(occ_size)]
    occ_from = [lax.rem(occ + occ_size - k, occ_size) for k in range(occ_size)]
    offsets = [divmod(k, occ_size) for k in range(devices - 1, 0, -1)]

    barrier = pltpu.get_barrier_semaphore()
    for dv, do in offsets:
        pl.semaphore_signal(
            barrier, inc=1, device_id={"vir": vir_to[dv], "occ": occ_to[do]},
            device_id_type=pl.DeviceIdType.MESH,
        )

    def block(z_to, y_to):
        first = (z_to * 2 + y_to) * own_rows
        return pl.ds(pl.multiple_of(first, own_rows), own_rows)

    middle = line // 2
    order = sorted(range(1, line), key=lambda s: abs(s - middle)) + [0]
    own_copies = {}
    for s in order:
        own_copies[s] = pltpu.make_async_copy(
            partial_ref.at[block((z + s) % line, y)], own.at[s], own_sem.at[s]
        )
        own_copies[s].start()
    pl.semaphore_wait(barrier, devices - 1)
    pair_copies = {}
    for s in order:
        pair_copies[s] = pltpu.make_async_remote_copy(
            src_ref=partial_ref.at[block((z + s) % line, 1 - y)],
            dst_ref=pair_in.at[s],
            send_sem=pair_send.at[s], recv_sem=pair_recv.at[s],
            device_id={"vir": z * 2 + 1 - y, "occ": occ},
            device_id_type=pl.DeviceIdType.MESH,
        )
        pair_copies[s].start()

    half = vir_size * a_fold * a_own
    lanes = occ_size * 128
    square = i_own * i_own

    def place_rows(at, r):
        fold, rest = quotient(at, half), remainder(at, half)
        v = quotient(rest, a_fold * a_own)
        p = remainder(quotient(rest, a_own), a_fold)
        b = remainder(rest, a_own)
        return r == (fold * a_fold + p) * NW + v * a_own + b

    def return_rows(r, at):
        fold, rest = quotient(at, half), remainder(at, half)
        v = quotient(rest, a_fold * a_own)
        p = remainder(quotient(rest, a_own), a_fold)
        b = remainder(rest, a_own)
        return r == b * NW + v * a_own + fold * a_fold + p

    rows_out[...] = one_hot((own_rows, own_rows), place_rows)
    rows_in[...] = one_hot((own_rows, own_rows), return_rows)
    for fold in range(folds):
        def place_cols(c, at):
            o, rest = quotient(at, 128), remainder(at, 128)
            j = quotient(remainder(rest, square), i_own)
            i = remainder(rest, i_own)
            return (quotient(rest, square) == fold) & (c == i * NO + o * i_own + j)

        def return_cols(at, c):
            o, rest = quotient(at, 128), remainder(at, 128)
            j = quotient(remainder(rest, square), i_own)
            i = remainder(rest, i_own)
            return (quotient(rest, square) == fold) & (c == j * NO + o * i_own + i)

        cols_out[fold] = one_hot((width, lanes), place_cols)
        cols_in[fold] = one_hot((lanes, width), return_cols)

    line_copies = {}
    for s in order:
        pair_copies[s].wait_recv()
        own_copies[s].wait()
        if s == 0:
            continue
        line_out[s] = own[s] + pair_in[s]
        line_copies[s] = pltpu.make_async_remote_copy(
            src_ref=line_out.at[s], dst_ref=line_in.at[s],
            send_sem=line_send.at[s], recv_sem=line_recv.at[s],
            device_id={"vir": ((z + s) % line) * 2 + y, "occ": occ},
            device_id_type=pl.DeviceIdType.MESH,
        )
        line_copies[s].start()
    total = own[0] + pair_in[0]
    for s in order[:-1]:
        line_copies[s].wait_recv()
        total = total + line_in[s]

    moved = permute_rows(rows_out[...], total)
    folded = permute_cols(moved[:half], cols_out[0])
    for fold in range(1, folds):
        folded = folded + permute_cols(moved[fold * half:(fold + 1) * half], cols_out[fold])
    outgoing[...] = folded

    def cell(ref, v, o):
        return ref.at[
            pl.ds(pl.multiple_of(v * 8, 8), 8), pl.ds(pl.multiple_of(o * 128, 128), 128)
        ]

    def mirror_copy(dv, do, v, o):
        k = dv * occ_size + do
        return pltpu.make_async_remote_copy(
            src_ref=cell(outgoing, vir_to[dv], occ_to[do]), dst_ref=cell(incoming, v, o),
            send_sem=mirror_send.at[k], recv_sem=mirror_recv.at[k],
            device_id={"vir": vir_to[dv], "occ": occ_to[do]},
            device_id_type=pl.DeviceIdType.MESH,
        )

    for dv, do in offsets:
        mirror_copy(dv, do, vir, occ).start()
    cell(incoming, vir, occ)[...] = cell(outgoing, vir, occ)[...]
    for dv, do in offsets:
        mirror_copy(dv, do, vir_from[dv], occ_from[do]).wait_recv()
    unfolded = [permute_cols(incoming[...], cols_in[fold]) for fold in range(folds)]
    out_ref[...] = total + permute_rows(rows_in[...], jnp.concatenate(unfolded, axis=0))

    for s in order:
        pair_copies[s].wait_send()
        if s:
            line_copies[s].wait_send()
    for dv, do in offsets:
        mirror_copy(dv, do, vir, occ).wait_send()


def exchange(partial_sum):
    vir_size, occ_size = lax.axis_size("vir"), lax.axis_size("occ")
    pair_rows, width = partial_sum.shape
    own_rows = pair_rows // vir_size
    line = vir_size // 2
    folds = 128 // (NO // occ_size) ** 2
    lanes = occ_size * 128
    block = (line, own_rows, width)
    devices = vir_size * occ_size
    return pl.pallas_call(
        functools.partial(exchange_kernel, vir_size, occ_size),
        out_shape=jax.ShapeDtypeStruct((own_rows, width), jnp.float32),
        in_specs=[pl.BlockSpec(memory_space=pl.ANY)],
        out_specs=pl.BlockSpec(memory_space=pltpu.VMEM),
        scratch_shapes=[
            pltpu.VMEM(block, jnp.float32),
            pltpu.VMEM(block, jnp.float32),
            pltpu.VMEM(block, jnp.float32),
            pltpu.VMEM(block, jnp.float32),
            pltpu.VMEM((vir_size * 8, lanes), jnp.float32),
            pltpu.VMEM((vir_size * 8, lanes), jnp.float32),
            pltpu.VMEM((own_rows, own_rows), jnp.bfloat16),
            pltpu.VMEM((folds, width, lanes), jnp.bfloat16),
            pltpu.VMEM((own_rows, own_rows), jnp.bfloat16),
            pltpu.VMEM((folds, lanes, width), jnp.bfloat16),
            pltpu.SemaphoreType.DMA((line,)),
            pltpu.SemaphoreType.DMA((line,)),
            pltpu.SemaphoreType.DMA((line,)),
            pltpu.SemaphoreType.DMA((line,)),
            pltpu.SemaphoreType.DMA((line,)),
            pltpu.SemaphoreType.DMA((devices,)),
            pltpu.SemaphoreType.DMA((devices,)),
        ],
        compiler_params=pltpu.CompilerParams(
            collective_id=0, has_side_effects=True, vmem_limit_bytes=24 * MIB
        ),
    )(partial_sum)


def exchange_by_collectives(partial_sum):
    pair_rows, ij_dev = partial_sum.shape
    occ_local = ij_dev // NO
    swapped = partial_sum.reshape(NW, NW, ij_dev).transpose(1, 0, 2).reshape(pair_rows, ij_dev)
    moved = lax.all_to_all(
        swapped.reshape(pair_rows, occ_local, NO), "occ", split_axis=2, concat_axis=1, tiled=True
    )
    numerator = partial_sum + moved.transpose(0, 2, 1).reshape(pair_rows, ij_dev)
    return lax.psum_scatter(numerator, "vir", scatter_dimension=0, tiled=True)


def per_device(tiles, tile_slot, amplitudes, occ_energy, vir_energy):
    ij_dev = amplitudes.shape[1]
    pair_rows = NW * NW
    row_blocks = pair_rows // tiles.shape[1]
    own_rows = pair_rows // lax.axis_size("vir")
    row_ids = lax.axis_index("vir") * own_rows + jnp.arange(own_rows)
    orbital = jnp.arange(NW)
    picks = (row_ids[:, None] // NW == orbital[None, :], row_ids[:, None] % NW == orbital[None, :])
    vir_pair = sum(jnp.sum(jnp.where(p, vir_energy[None, :], 0.0), axis=1) for p in picks)
    col_ids = lax.axis_index("occ") * ij_dev + jnp.arange(ij_dev)
    occupied = jnp.arange(NO)
    picks = (col_ids[None, :] // NO == occupied[:, None], col_ids[None, :] % NO == occupied[:, None])
    occ_pair = sum(jnp.sum(jnp.where(p, occ_energy[:, None], 0.0), axis=0) for p in picks)
    partial_sum = ladder_partial(tiles, tile_slot, amplitudes, row_blocks)
    if mirror_fits(lax.axis_size("vir"), lax.axis_size("occ")):
        numerator = exchange(partial_sum)
    else:
        numerator = exchange_by_collectives(partial_sum)
    return numerator / (occ_pair[None, :] - vir_pair[:, None])


def solution(mesh):
    in_specs = (P("vir", None, None), P("vir"), P("vir", "occ"), P(), P())
    out_specs = P("vir", "occ")
    return jax.shard_map(
        per_device, mesh=mesh, in_specs=in_specs, out_specs=out_specs, check_vma=False
    )
```

```python
import functools

import jax
import jax.numpy as jnp
from jax import lax
from jax.experimental import pallas as pl
from jax.experimental.pallas import tpu as pltpu
from jax.sharding import PartitionSpec as P

NO = 32
NW = 32
GROUP = 4
UNROLL = 4
TILE_DEPTH = 6
AMP_PARTS = 8
MIB = 1024 * 1024


def split_two(x):
    high = x.astype(jnp.bfloat16)
    low = (x - high.astype(jnp.float32)).astype(jnp.bfloat16)
    return high, low


def quotient(x, n):
    if n & (n - 1) == 0:
        return x >> (n.bit_length() - 1)
    return x // n


def remainder(x, n):
    if n & (n - 1) == 0:
        return x & (n - 1)
    return x % n


def ladder_kernel(
    row_blocks, slots_ref, slot_vec_ref, tiles_hbm, amp_hbm, out_ref,
    amp, ring, places, cursor,
    amp_sem, ring_sem,
):
    slot_count, tile, _ = tiles_hbm.shape
    cd, width = amp_hbm.shape
    col_blocks = cd // tile
    batch = GROUP * UNROLL
    row_bits, col_bits = row_blocks.bit_length(), col_blocks.bit_length()

    part = cd // AMP_PARTS

    def amp_copy(i):
        rows = pl.ds(i * part, part)
        return pltpu.make_async_copy(amp_hbm.at[rows], amp.at[rows], amp_sem.at[i])

    for i in range(AMP_PARTS):
        amp_copy(i).start()

    slot_vec = slot_vec_ref[...]
    start = jnp.int32(0)
    for r in range(row_blocks):
        inside = (slot_vec >= r * col_blocks) & (slot_vec < (r + 1) * col_blocks)
        count = jnp.sum(jnp.where(inside, 1.0, 0.0)).astype(jnp.int32)
        cursor[r] = start
        start = start + ((count + GROUP - 1) // GROUP) * GROUP
        for t in range(1, GROUP):
            at = jnp.maximum(start - t, 0)
            places[at] = col_blocks
    total = start
    for t in range(batch):
        places[total + t] = col_blocks
    cursor[row_blocks] = total + batch
    steps = (total + batch - 1) // batch

    out_ref[...] = jnp.zeros_like(out_ref)
    amp[pl.ds(cd, tile), :] = jnp.zeros((tile, width), jnp.float32)

    def place(i, carry):
        for q in range(8):
            k = i * 8 + q
            s = slots_ref[k]
            r = quotient(s, col_blocks)
            at = cursor[r]
            places[at] = (((k << row_bits) + r) << col_bits) + (s - r * col_blocks)
            cursor[r] = at + 1
        return carry

    lax.fori_loop(0, slot_count // 8, place, 0)

    def start_tiles(i):
        slot = lax.rem(i, TILE_DEPTH)
        for t in range(batch):
            pltpu.make_async_copy(
                tiles_hbm.at[places[i * batch + t] >> (row_bits + col_bits)],
                ring.at[slot, t], ring_sem.at[slot],
            ).start()

    def wait_tiles(i):
        slot = lax.rem(i, TILE_DEPTH)
        pltpu.make_async_copy(
            tiles_hbm.at[pl.ds(0, batch)], ring.at[slot], ring_sem.at[slot]
        ).wait()

    for i in range(TILE_DEPTH - 1):
        @pl.when(i < steps)
        def _(i=i):
            start_tiles(jnp.int32(i))
    for i in range(AMP_PARTS):
        amp_copy(i).wait()

    def multiply(i, carry):
        wait_tiles(i)

        @pl.when(i + TILE_DEPTH - 1 < steps)
        def _():
            start_tiles(i + TILE_DEPTH - 1)

        slot = lax.rem(i, TILE_DEPTH)
        products = []
        for u in range(UNROLL):
            highs, lows, amp_highs, amp_lows = [], [], [], []
            for t in range(GROUP):
                at = u * GROUP + t
                high, low = split_two(ring[slot, at])
                col = places[i * batch + at] & ((1 << col_bits) - 1)
                first = pl.multiple_of(col * tile, tile)
                highs.append(high)
                lows.append(low)
                amp_high, amp_low = split_two(amp[pl.ds(first, tile), :])
                amp_highs.append(amp_high)
                amp_lows.append(amp_low)
            left = jnp.concatenate(highs + lows + highs, axis=1)
            right = jnp.concatenate(amp_highs + amp_highs + amp_lows, axis=0)
            products.append(jnp.dot(left, right, preferred_element_type=jnp.float32))
        for u in range(UNROLL):
            row = (places[i * batch + u * GROUP] >> col_bits) & ((1 << row_bits) - 1)
            first = pl.multiple_of(row * tile, tile)
            out_ref[pl.ds(first, tile), :] += products[u]
        return carry

    lax.fori_loop(0, steps, multiply, 0)


def ladder_partial(tiles, tile_slot, amplitudes, row_blocks):
    slot_count, tile, _ = tiles.shape
    cd, width = amplitudes.shape
    batch = GROUP * UNROLL
    lanes = min(128, slot_count)
    places = 2 * slot_count + row_blocks * GROUP + 2 * batch
    flops = 6 * slot_count * tile * tile * width
    return pl.pallas_call(
        functools.partial(ladder_kernel, row_blocks),
        out_shape=jax.ShapeDtypeStruct((row_blocks * tile, width), jnp.float32),
        in_specs=[
            pl.BlockSpec(memory_space=pltpu.SMEM),
            pl.BlockSpec(memory_space=pltpu.VMEM),
            pl.BlockSpec(memory_space=pl.ANY),
            pl.BlockSpec(memory_space=pl.ANY),
        ],
        out_specs=pl.BlockSpec(memory_space=pltpu.VMEM),
        scratch_shapes=[
            pltpu.VMEM((cd + tile, width), jnp.float32),
            pltpu.VMEM((TILE_DEPTH, batch, tile, tile), jnp.float32),
            pltpu.SMEM((places,), jnp.int32),
            pltpu.SMEM((row_blocks + 1,), jnp.int32),
            pltpu.SemaphoreType.DMA((AMP_PARTS,)),
            pltpu.SemaphoreType.DMA((TILE_DEPTH,)),
        ],
        compiler_params=pltpu.CompilerParams(vmem_limit_bytes=56 * MIB),
        cost_estimate=pl.CostEstimate(
            flops=flops,
            bytes_accessed=4 * (tiles.size + amplitudes.size),
            transcendentals=0,
        ),
    )(tile_slot, tile_slot.reshape(slot_count // lanes, lanes), tiles, amplitudes)


def one_hot(shape, want):
    row = lax.broadcasted_iota(jnp.int32, shape, 0)
    col = lax.broadcasted_iota(jnp.int32, shape, 1)
    return jnp.where(want(row, col), 1.0, 0.0).astype(jnp.bfloat16)


def three_terms(x):
    first = x.astype(jnp.bfloat16)
    rest = x - first.astype(jnp.float32)
    second = rest.astype(jnp.bfloat16)
    third = (rest - second.astype(jnp.float32)).astype(jnp.bfloat16)
    return [first, second, third]


def permute_rows(rows, x):
    width = x.shape[1]
    wide = jnp.dot(
        rows, jnp.concatenate(three_terms(x), axis=1), preferred_element_type=jnp.float32
    )
    return wide[:, :width] + wide[:, width:2 * width] + wide[:, 2 * width:]


def permute_cols(x, cols):
    depth = x.shape[0]
    tall = jnp.dot(
        jnp.concatenate(three_terms(x), axis=0), cols, preferred_element_type=jnp.float32
    )
    return tall[:depth] + tall[depth:2 * depth] + tall[2 * depth:]


def mirror_fits(vir_size, occ_size):
    if vir_size % 2 or NW % vir_size or NO % occ_size:
        return False
    a_own, i_own = NW // vir_size, NO // occ_size
    if 128 % (i_own * i_own) or a_own * a_own * i_own * i_own != 1024:
        return False
    return a_own % (128 // (i_own * i_own)) == 0


def exchange_kernel(
    vir_size, occ_size, partial_ref, out_ref,
    own, pair_in, line_out, line_in, outgoing, incoming,
    rows_out, cols_out, rows_in, cols_in,
    own_sem, pair_send, pair_recv, line_send, line_recv, mirror_send, mirror_recv,
):
    own_rows, width = out_ref.shape
    a_own, i_own = NW // vir_size, NO // occ_size
    folds = 128 // (i_own * i_own)
    a_fold = a_own // folds
    devices = vir_size * occ_size
    line = vir_size // 2
    vir = lax.axis_index("vir")
    occ = lax.axis_index("occ")
    z, y = vir // 2, vir % 2
    vir_to = [lax.rem(vir + k, vir_size) for k in range(vir_size)]
    vir_from = [lax.rem(vir + vir_size - k, vir_size) for k in range(vir_size)]
    occ_to = [lax.rem(occ + k, occ_size) for k in range(occ_size)]
    occ_from = [lax.rem(occ + occ_size - k, occ_size) for k in range(occ_size)]
    offsets = [divmod(k, occ_size) for k in range(devices - 1, 0, -1)]

    barrier = pltpu.get_barrier_semaphore()
    for dv, do in offsets:
        pl.semaphore_signal(
            barrier, inc=1, device_id={"vir": vir_to[dv], "occ": occ_to[do]},
            device_id_type=pl.DeviceIdType.MESH,
        )

    def block(z_to, y_to):
        first = (z_to * 2 + y_to) * own_rows
        return pl.ds(pl.multiple_of(first, own_rows), own_rows)

    middle = line // 2
    order = sorted(range(1, line), key=lambda s: abs(s - middle)) + [0]
    own_copies = {}
    for s in order:
        own_copies[s] = pltpu.make_async_copy(
            partial_ref.at[block((z + s) % line, y)], own.at[s], own_sem.at[s]
        )
        own_copies[s].start()
    pl.semaphore_wait(barrier, devices - 1)
    pair_copies = {}
    for s in order:
        pair_copies[s] = pltpu.make_async_remote_copy(
            src_ref=partial_ref.at[block((z + s) % line, 1 - y)],
            dst_ref=pair_in.at[s],
            send_sem=pair_send.at[s], recv_sem=pair_recv.at[s],
            device_id={"vir": z * 2 + 1 - y, "occ": occ},
            device_id_type=pl.DeviceIdType.MESH,
        )
        pair_copies[s].start()

    half = vir_size * a_fold * a_own
    lanes = occ_size * 128
    square = i_own * i_own

    def place_rows(at, r):
        fold, rest = quotient(at, half), remainder(at, half)
        v = quotient(rest, a_fold * a_own)
        p = remainder(quotient(rest, a_own), a_fold)
        b = remainder(rest, a_own)
        return r == (fold * a_fold + p) * NW + v * a_own + b

    def return_rows(r, at):
        fold, rest = quotient(at, half), remainder(at, half)
        v = quotient(rest, a_fold * a_own)
        p = remainder(quotient(rest, a_own), a_fold)
        b = remainder(rest, a_own)
        return r == b * NW + v * a_own + fold * a_fold + p

    rows_out[...] = one_hot((own_rows, own_rows), place_rows)
    rows_in[...] = one_hot((own_rows, own_rows), return_rows)
    for fold in range(folds):
        def place_cols(c, at):
            o, rest = quotient(at, 128), remainder(at, 128)
            j = quotient(remainder(rest, square), i_own)
            i = remainder(rest, i_own)
            return (quotient(rest, square) == fold) & (c == i * NO + o * i_own + j)

        def return_cols(at, c):
            o, rest = quotient(at, 128), remainder(at, 128)
            j = quotient(remainder(rest, square), i_own)
            i = remainder(rest, i_own)
            return (quotient(rest, square) == fold) & (c == j * NO + o * i_own + i)

        cols_out[fold] = one_hot((width, lanes), place_cols)
        cols_in[fold] = one_hot((lanes, width), return_cols)

    line_copies = {}
    for s in order:
        pair_copies[s].wait_recv()
        own_copies[s].wait()
        if s == 0:
            continue
        line_out[s] = own[s] + pair_in[s]
        line_copies[s] = pltpu.make_async_remote_copy(
            src_ref=line_out.at[s], dst_ref=line_in.at[s],
            send_sem=line_send.at[s], recv_sem=line_recv.at[s],
            device_id={"vir": ((z + s) % line) * 2 + y, "occ": occ},
            device_id_type=pl.DeviceIdType.MESH,
        )
        line_copies[s].start()
    total = own[0] + pair_in[0]
    for s in order[:-1]:
        line_copies[s].wait_recv()
        total = total + line_in[s]

    moved = permute_rows(rows_out[...], total)
    folded = permute_cols(moved[:half], cols_out[0])
    for fold in range(1, folds):
        folded = folded + permute_cols(moved[fold * half:(fold + 1) * half], cols_out[fold])
    outgoing[...] = folded

    def cell(ref, v, o):
        return ref.at[
            pl.ds(pl.multiple_of(v * 8, 8), 8), pl.ds(pl.multiple_of(o * 128, 128), 128)
        ]

    def mirror_copy(dv, do, v, o):
        k = dv * occ_size + do
        return pltpu.make_async_remote_copy(
            src_ref=cell(outgoing, vir_to[dv], occ_to[do]), dst_ref=cell(incoming, v, o),
            send_sem=mirror_send.at[k], recv_sem=mirror_recv.at[k],
            device_id={"vir": vir_to[dv], "occ": occ_to[do]},
            device_id_type=pl.DeviceIdType.MESH,
        )

    for dv, do in offsets:
        mirror_copy(dv, do, vir, occ).start()
    cell(incoming, vir, occ)[...] = cell(outgoing, vir, occ)[...]
    for dv, do in offsets:
        mirror_copy(dv, do, vir_from[dv], occ_from[do]).wait_recv()
    unfolded = [permute_cols(incoming[...], cols_in[fold]) for fold in range(folds)]
    out_ref[...] = total + permute_rows(rows_in[...], jnp.concatenate(unfolded, axis=0))

    for s in order:
        pair_copies[s].wait_send()
        if s:
            line_copies[s].wait_send()
    for dv, do in offsets:
        mirror_copy(dv, do, vir, occ).wait_send()


def exchange(partial_sum):
    vir_size, occ_size = lax.axis_size("vir"), lax.axis_size("occ")
    pair_rows, width = partial_sum.shape
    own_rows = pair_rows // vir_size
    line = vir_size // 2
    folds = 128 // (NO // occ_size) ** 2
    lanes = occ_size * 128
    block = (line, own_rows, width)
    devices = vir_size * occ_size
    return pl.pallas_call(
        functools.partial(exchange_kernel, vir_size, occ_size),
        out_shape=jax.ShapeDtypeStruct((own_rows, width), jnp.float32),
        in_specs=[pl.BlockSpec(memory_space=pl.ANY)],
        out_specs=pl.BlockSpec(memory_space=pltpu.VMEM),
        scratch_shapes=[
            pltpu.VMEM(block, jnp.float32),
            pltpu.VMEM(block, jnp.float32),
            pltpu.VMEM(block, jnp.float32),
            pltpu.VMEM(block, jnp.float32),
            pltpu.VMEM((vir_size * 8, lanes), jnp.float32),
            pltpu.VMEM((vir_size * 8, lanes), jnp.float32),
            pltpu.VMEM((own_rows, own_rows), jnp.bfloat16),
            pltpu.VMEM((folds, width, lanes), jnp.bfloat16),
            pltpu.VMEM((own_rows, own_rows), jnp.bfloat16),
            pltpu.VMEM((folds, lanes, width), jnp.bfloat16),
            pltpu.SemaphoreType.DMA((line,)),
            pltpu.SemaphoreType.DMA((line,)),
            pltpu.SemaphoreType.DMA((line,)),
            pltpu.SemaphoreType.DMA((line,)),
            pltpu.SemaphoreType.DMA((line,)),
            pltpu.SemaphoreType.DMA((devices,)),
            pltpu.SemaphoreType.DMA((devices,)),
        ],
        compiler_params=pltpu.CompilerParams(
            collective_id=0, has_side_effects=True, vmem_limit_bytes=24 * MIB
        ),
    )(partial_sum)


def exchange_by_collectives(partial_sum):
    pair_rows, ij_dev = partial_sum.shape
    occ_local = ij_dev // NO
    swapped = partial_sum.reshape(NW, NW, ij_dev).transpose(1, 0, 2).reshape(pair_rows, ij_dev)
    moved = lax.all_to_all(
        swapped.reshape(pair_rows, occ_local, NO), "occ", split_axis=2, concat_axis=1, tiled=True
    )
    numerator = partial_sum + moved.transpose(0, 2, 1).reshape(pair_rows, ij_dev)
    return lax.psum_scatter(numerator, "vir", scatter_dimension=0, tiled=True)


def per_device(tiles, tile_slot, amplitudes, occ_energy, vir_energy):
    ij_dev = amplitudes.shape[1]
    pair_rows = NW * NW
    row_blocks = pair_rows // tiles.shape[1]
    own_rows = pair_rows // lax.axis_size("vir")
    row_ids = lax.axis_index("vir") * own_rows + jnp.arange(own_rows)
    orbital = jnp.arange(NW)
    picks = (row_ids[:, None] // NW == orbital[None, :], row_ids[:, None] % NW == orbital[None, :])
    vir_pair = sum(jnp.sum(jnp.where(p, vir_energy[None, :], 0.0), axis=1) for p in picks)
    col_ids = lax.axis_index("occ") * ij_dev + jnp.arange(ij_dev)
    occupied = jnp.arange(NO)
    picks = (col_ids[None, :] // NO == occupied[:, None], col_ids[None, :] % NO == occupied[:, None])
    occ_pair = sum(jnp.sum(jnp.where(p, occ_energy[:, None], 0.0), axis=0) for p in picks)
    partial_sum = ladder_partial(tiles, tile_slot, amplitudes, row_blocks)
    if mirror_fits(lax.axis_size("vir"), lax.axis_size("occ")):
        numerator = exchange(partial_sum)
    else:
        numerator = exchange_by_collectives(partial_sum)
    return numerator / (occ_pair[None, :] - vir_pair[:, None])


def solution(mesh):
    in_specs = (P("vir", None, None), P("vir"), P("vir", "occ"), P(), P())
    out_specs = P("vir", "occ")
    return jax.shard_map(
        per_device, mesh=mesh, in_specs=in_specs, out_specs=out_specs, check_vma=False
    )
```
